256 devices in a mesh: seq: 32 (over y, x, core), kvh: 8 (over z).
Axes of the slice: x: 4, y: 4, z: 8, core: 2. Of those that a mesh axis runs over, the one named last changes fastest.
Arguments:
- query: bfloat16 [4, 128, 128], P(None, 'kvh'), may hold values from -4 to 4
- key_cache: bfloat16 [4, 16384, 8, 128], P(None, 'seq', 'kvh'), may hold values from -5.5 to 5.5
- value_cache: bfloat16 [4, 16384, 8, 128], P(None, 'seq', 'kvh'), may hold values from -5 to 5
- lengths: int32 [4], replicated, may hold values from 8192 to 16384, as said below
- residual: float32 [4, 16384], P(None, ('seq', 'kvh')), may hold values from -32 to 32
- out_weight: bfloat16 [8, 2048, 16384], P('kvh', 'seq'), may hold values from -0.09375 to 0.09375
- norm_gain: float32 [16384], P('seq'), may hold values from 0.25 to 1.75
- gate_weight: bfloat16 [16384, 26624], P('seq', 'kvh'), may hold values from -0.046875 to 0.046875
- up_weight: bfloat16 [16384, 26624], P('seq', 'kvh'), may hold values from -0.046875 to 0.046875
- down_weight: bfloat16 [26624, 16384], P('kvh', 'seq'), may hold values from -0.0625 to 0.0625
Outputs:
- next_hidden: float32 [4, 16384], P(None, ('seq', 'kvh'))
The draws below stay inside these ranges and needn't reach their ends.
Inputs may be any that keep to these rules, and one draw needn't show every extreme that they name: `lengths`: each a multiple of 128; one request has exactly 16384 and one exactly 8192.
All inputs are finite; a program needn't handle non-finite values.
Results may differ from the reference program's by a relative error of at most 0.0017.
Values may be sent and summed in bfloat16 or wider, within the bound.
No kernel may reach another device: no remote copies, remote signals or barrier semaphores. Data moves between devices by JAX's collectives and lax.ppermute only.
A program may use at most 64 MiB of HBM per device.

```python
import math
import jax
import jax.numpy as jnp
from jax import lax

D = 16384
HEAD_DIM = 128
GROUP_HEADS = 16
FF_W = 26624
REQUESTS = 4
KV_HEADS = 8
HEADS = 128
CTX = 16384


def draw_query(key, part):
    key = jax.random.fold_in(key, 1)
    values = jax.random.truncated_normal(key, -4.0, 4.0, (REQUESTS, HEADS, HEAD_DIM), jnp.float32)
    return values.astype(jnp.bfloat16)


def draw_key_cache(key, part):
    key = jax.random.fold_in(key, 2)
    values = jax.random.truncated_normal(key, -4.0, 4.0, (REQUESTS, CTX, KV_HEADS, HEAD_DIM), jnp.float32)
    return values.astype(jnp.bfloat16)


def draw_value_cache(key, part):
    key = jax.random.fold_in(key, 3)
    key_amp, key_phase, key_noise = jax.random.split(key, 3)
    amplitude = jnp.exp(jax.random.uniform(key_amp, (REQUESTS, 1, KV_HEADS, HEAD_DIM), jnp.float32, math.log(0.8), math.log(2.5)))
    phase = jax.random.uniform(key_phase, (REQUESTS, 1, KV_HEADS, HEAD_DIM), jnp.float32, -math.pi, math.pi)
    positions = jnp.arange(CTX, dtype=jnp.float32)[None, :, None, None]
    wave = amplitude * jnp.sin(positions * (3.0 * math.pi / CTX) + phase)
    noise = 0.6 * jax.random.truncated_normal(key_noise, -4.0, 4.0, (REQUESTS, CTX, KV_HEADS, HEAD_DIM), jnp.float32)
    return (wave + noise).astype(jnp.bfloat16)


def draw_lengths(key, part):
    key = jax.random.fold_in(key, 4)
    key_units, key_order = jax.random.split(key, 2)
    half_units = CTX // 256
    full_units = CTX // 128
    units = jax.random.randint(key_units, (REQUESTS,), half_units, full_units + 1)
    order = jax.random.permutation(key_order, REQUESTS)
    units = jnp.where(order == 0, full_units, jnp.where(order == 1, half_units, units))
    return (units * 128).astype(jnp.int32)


def draw_residual(key, part):
    key = jax.random.fold_in(key, 5)
    key_values, key_spread = jax.random.split(key, 2)
    columns = jnp.arange(D, dtype=jnp.float32)[None, :]
    spread = jnp.exp(jax.random.uniform(key_spread, (1, D), jnp.float32, 0.0, math.log(3.0)))
    column_scale = (0.5 + columns / D) * spread
    values = jax.random.truncated_normal(key_values, -4.0, 4.0, (REQUESTS, D), jnp.float32)
    return (values * column_scale).astype(jnp.float32)


def spiked(drawn, stream_key, source, target, blocks, factor):
    owner, partner = [(jnp.arange(drawn.shape[position]) // (drawn.shape[position] // blocks)).reshape([-1 if axis == position else 1 for axis in range(drawn.ndim)]) for position in (source, target)]
    chosen = jax.random.permutation(stream_key, blocks)[partner]
    strong = (owner == chosen) | (owner == (partner + blocks // 2) % blocks)
    return jnp.where(strong, factor * drawn, drawn)


def block_levels(key, extent, shards, smallest, high):
    gain, own = 1.0, jax.random.fold_in(key, 6)
    for position, parts in shards:
        heights = jnp.exp(jax.random.uniform(jax.random.fold_in(own, position), (parts,), jnp.float32, smallest / len(shards), high / len(shards)))
        gain = gain * jnp.repeat(heights, extent[position] // parts).reshape([-1 if axis == position else 1 for axis in range(len(extent))])
    return gain


def scatter_about(rng, extent, scale, bound, pieces=(), kind=jnp.bfloat16):
    array = scale * jax.random.normal(rng, extent, jnp.float32)
    if pieces:
        array = array * block_levels(rng, extent, pieces, -0.22, 0.18)
    return jnp.clip(array, -bound, bound).astype(kind)


def bell_draw_with(stream_key, shape, scale, bound, cuts, heavy, held_as=jnp.bfloat16):
    values = scale * jax.random.normal(stream_key, shape, jnp.float32)
    if cuts:
        values = values * block_levels(stream_key, shape, cuts, -0.22, 0.18)
    return jnp.clip(spiked(values, jax.random.fold_in(stream_key, 3), *heavy), -bound, bound).astype(held_as)


def setup_inputs(seed: int = 0) -> dict:
    key_of = jax.random.split(jax.random.key(seed), 11)
    return {
        "query": draw_query(jax.random.fold_in(key_of[10], 71), 0),
        "key_cache": draw_key_cache(jax.random.fold_in(key_of[10], 71), 0),
        "value_cache": draw_value_cache(jax.random.fold_in(key_of[10], 71), 0),
        "lengths": draw_lengths(jax.random.fold_in(key_of[10], 71), 0),
        "residual": draw_residual(jax.random.fold_in(key_of[10], 71), 0),
        "out_weight": bell_draw_with(key_of[5], (KV_HEADS, GROUP_HEADS * HEAD_DIM, D), (HEADS * HEAD_DIM) ** -0.5, 0.09375, ((0, 8), (1, 32)), (1, 2, 32, 2.75)),
        "norm_gain": jnp.clip(1.0 + 0.15 * jax.random.normal(key_of[6], (D,), jnp.float32), 0.25, 1.75),
        "gate_weight": scatter_about(key_of[7], (D, FF_W), D ** -0.5, 0.046875, ((0, 32), (1, 8))),
        "up_weight": scatter_about(key_of[8], (D, FF_W), D ** -0.5, 0.046875, ((0, 32), (1, 8))),
        "down_weight": bell_draw_with(key_of[9], (FF_W, D), FF_W ** -0.5, 0.0625, ((0, 8), (1, 32)), (0, 1, 32, 2.75)),
    }


EPSILON = 1e-05
MASKED = -1e+30

def group_attention(query, key_cache, value_cache, lengths, group):
    keys = key_cache[:, :, group, :].astype(jnp.float32)
    values = value_cache[:, :, group, :].astype(jnp.float32)
    queries = query[:, group * GROUP_HEADS:(group + 1) * GROUP_HEADS, :].astype(jnp.float32)
    scores = jnp.einsum('bhd,bpd->bhp', queries, keys, precision=lax.Precision.HIGHEST) * HEAD_DIM ** (-0.5)
    positions = jnp.arange(CTX, dtype=jnp.int32)
    live = positions[None, None, :] < lengths[:, None, None]
    masked = jnp.where(live, scores, MASKED)
    top = lax.optimization_barrier(jnp.max(masked, axis=2, keepdims=True))
    weights = jnp.where(live, jnp.exp(masked - top), 0.0)
    summed = jnp.einsum('bhp,bpd->bhd', weights, values, precision=lax.Precision.HIGHEST)
    return (summed / lax.optimization_barrier(jnp.sum(weights, axis=2))[:, :, None]).astype(jnp.bfloat16)

def reference(query, key_cache, value_cache, lengths, residual, out_weight, norm_gain, gate_weight, up_weight, down_weight):
    projected = jnp.zeros((REQUESTS, D), jnp.float32)
    for group in range(KV_HEADS):
        attention = group_attention(query, key_cache, value_cache, lengths, group)
        attention = attention.reshape(REQUESTS, GROUP_HEADS * HEAD_DIM)
        projected = projected + jnp.dot(attention, out_weight[group], preferred_element_type=jnp.float32)
    carried = residual + projected
    scale_rows = lax.rsqrt(lax.optimization_barrier(jnp.mean(carried * carried, axis=1)) + EPSILON)
    normed = (carried * scale_rows[:, None] * norm_gain[None, :]).astype(jnp.bfloat16)
    gate = jnp.dot(normed, gate_weight, preferred_element_type=jnp.float32)
    up = jnp.dot(normed, up_weight, preferred_element_type=jnp.float32)
    activated = (jax.nn.silu(gate) * up).astype(jnp.bfloat16)
    return carried + jnp.dot(activated, down_weight, preferred_element_type=jnp.float32)
```

```python
import jax
import jax.numpy as jnp
from jax import lax
from jax.experimental import pallas as pl
from jax.experimental.pallas import tpu as pltpu
from jax.sharding import PartitionSpec as P

EPSILON = 1e-05
MASKED = -1e30
LANES = 128
F32 = jnp.float32
BF16 = jnp.bfloat16


def dot(a, b):
    return jnp.dot(a, b, preferred_element_type=F32)


def attend_kernel(lengths, query, keys, values, out):
    batch, heads, head_dim = query.shape
    positions_here = keys.shape[1]
    pieces = out.shape[0]
    per_head = pieces // heads
    width = head_dim // per_head
    stat = (LANES - width) // 2
    first = lax.axis_index("seq") * positions_here
    positions = first + lax.broadcasted_iota(jnp.int32, (heads, positions_here), 1)
    for b in range(batch):
        scores = lax.dot_general(
            query[b], keys[b], (((1,), (1,)), ((), ())), preferred_element_type=F32
        ) * head_dim ** (-0.5)
        live = positions < lengths[b]
        masked = jnp.where(live, scores, MASKED)
        top = jnp.max(masked, axis=1, keepdims=True)
        weights = jnp.where(live, jnp.exp(masked - top), 0.0)
        total = jnp.sum(weights, axis=1, keepdims=True)
        high = weights.astype(BF16)
        low = (weights - high.astype(F32)).astype(BF16)
        both = dot(jnp.concatenate([high, low], axis=0), values[b])
        sums = both[:heads] + both[heads:]
        stats = jnp.concatenate(
            [jnp.broadcast_to(top, (heads, stat)), jnp.broadcast_to(total, (heads, stat))], axis=1
        )
        for part in range(per_head):
            packed = jnp.concatenate([sums[:, part * width : (part + 1) * width], stats], axis=1)
            for h in range(heads):
                out[h * per_head + part, b : b + 1, :] = packed[h : h + 1]


def project_kernel(parts, weight, out):
    width = weight.shape[0]
    stat = (LANES - width) // 2
    got = parts[...]
    top = jnp.max(got[:, :, width : width + 1], axis=0)
    factor = jnp.exp(got[:, :, width : width + 1] - top[None])
    total = jnp.sum(factor * got[:, :, width + stat : width + stat + 1], axis=0)
    merged = jnp.sum(factor * got[:, :, :width], axis=0)
    attention = (merged / total).astype(BF16)
    columns = out.shape[2]
    for piece in range(out.shape[0]):
        out[piece] = dot(attention, weight[:, piece * columns : (piece + 1) * columns])


def column_mask(shape, width):
    group = lax.axis_index("kvh")
    lanes = lax.broadcasted_iota(jnp.int32, shape, len(shape) - 1)
    return (lanes >= group * width) & (lanes < (group + 1) * width)


def carry_kernel(parts, residual, out):
    summed = jnp.sum(parts[...], axis=0)
    spread = jnp.concatenate([residual[...]] * (summed.shape[1] // residual.shape[1]), axis=1)
    summed = summed + jnp.where(column_mask(summed.shape, residual.shape[1]), spread, 0.0)
    for piece in range(out.shape[0]):
        out[piece] = summed


def gate_kernel(parts, gain, gate_weight, up_weight, out, carried_out):
    batch = parts.shape[1]
    carried = jnp.sum(parts[...], axis=0)
    width = carried_out.shape[1]
    own = jnp.where(column_mask(carried.shape, width), carried, 0.0)
    carried_out[...] = sum(
        own[:, piece * width : (piece + 1) * width] for piece in range(carried.shape[1] // width)
    )
    squares = jnp.broadcast_to(
        jnp.sum(carried * carried, axis=1, keepdims=True), (batch, LANES)
    )
    scaled = (carried * gain[...]).astype(BF16)
    zeros = jnp.zeros((batch, LANES), F32)
    tiles = gate_weight.shape[1] // LANES
    for tile in range(out.shape[0]):
        if tile < tiles:
            lanes = slice(tile * LANES, (tile + 1) * LANES)
            gate = dot(scaled, gate_weight[:, lanes])
            up = dot(scaled, up_weight[:, lanes])
        else:
            gate = up = zeros
        out[tile] = jnp.concatenate([gate, up, squares, zeros], axis=0)


def activate_kernel(width, parts, out):
    batch = out.shape[1]
    summed = jnp.sum(parts[...], axis=0)
    scale = lax.rsqrt(summed[2 * batch : 3 * batch] / width + EPSILON)
    gate = summed[:batch] * scale
    up = summed[batch : 2 * batch] * scale
    activated = (gate / (1.0 + jnp.exp(-gate)) * up).astype(BF16).astype(F32)
    for piece in range(out.shape[0]):
        out[piece] = activated


def down_kernel(activated, weight, out):
    tiles = weight.shape[0] // LANES
    full = jnp.concatenate([activated[tile] for tile in range(tiles)], axis=1).astype(BF16)
    down = dot(full, weight[...])
    pieces = out.shape[0]
    width = down.shape[1] // pieces
    per_tile = LANES // width
    for piece in range(pieces):
        tile = down[:, piece // per_tile * LANES : (piece // per_tile + 1) * LANES]
        shift = piece % per_tile * width
        out[piece] = tile if shift == 0 else pltpu.roll(tile, LANES - shift, 1)


def finish_kernel(parts, carried, out):
    out[...] = carried[...] + jnp.sum(parts[...], axis=0)[:, : out.shape[1]]


VMEM = pl.BlockSpec(memory_space=pltpu.VMEM)
SMEM = pl.BlockSpec(memory_space=pltpu.SMEM)


def call(kernel, shapes, specs, *args):
    return pl.pallas_call(
        kernel,
        out_shape=shapes,
        in_specs=specs,
        out_specs=jax.tree.map(lambda _: VMEM, shapes),
        compiler_params=pltpu.CompilerParams(vmem_limit_bytes=24 * 1024 * 1024),
    )(*args)


def swap(array, axis):
    return lax.all_to_all(array, axis, split_axis=0, concat_axis=0, tiled=True)


def on_device(
    query,
    key_cache,
    value_cache,
    lengths,
    residual,
    out_weight,
    norm_gain,
    gate_weight,
    up_weight,
    down_weight,
):
    seq_count = lax.axis_size("seq")
    kvh_count = lax.axis_size("kvh")
    batch = query.shape[0]
    columns = norm_gain.shape[0]
    own = residual.shape[1]

    def shape(*dims):
        return jax.ShapeDtypeStruct(dims, F32)

    with jax.named_scope("attend"):
        partial = call(
            attend_kernel,
            shape(seq_count, batch, LANES),
            [SMEM, VMEM, VMEM, VMEM],
            lengths,
            query,
            key_cache[:, :, 0, :],
            value_cache[:, :, 0, :],
        )
    partial = swap(partial, "seq")
    with jax.named_scope("project"):
        projected = call(
            project_kernel, shape(seq_count, batch, columns), [VMEM] * 2, partial, out_weight[0]
        )
    projected = swap(projected, "seq")
    with jax.named_scope("carry"):
        carried = call(
            carry_kernel, shape(kvh_count, batch, columns), [VMEM] * 2, projected, residual
        )
    carried = swap(carried, "kvh")
    with jax.named_scope("gate_up"):
        hidden, own_carried = call(
            gate_kernel,
            (shape(seq_count, 4 * batch, LANES), shape(batch, own)),
            [VMEM] * 4,
            carried,
            norm_gain.reshape(1, columns),
            gate_weight,
            up_weight,
        )
    hidden = swap(hidden, "seq")
    with jax.named_scope("activate"):
        width = seq_count * columns
        activated = call(
            lambda parts, out: activate_kernel(width, parts, out),
            shape(seq_count, batch, LANES),
            [VMEM],
            hidden,
        )
    activated = swap(activated, "seq")
    with jax.named_scope("down"):
        down = call(down_kernel, shape(kvh_count, batch, LANES), [VMEM] * 2, activated, down_weight)
    down = swap(down, "kvh")
    with jax.named_scope("finish"):
        return call(finish_kernel, shape(batch, own), [VMEM] * 2, down, own_carried)


def solution(mesh):
    return jax.shard_map(
        on_device,
        mesh=mesh,
        in_specs=(
            P(None, "kvh", None),
            P(None, "seq", "kvh", None),
            P(None, "seq", "kvh", None),
            P(),
            P(None, ("seq", "kvh")),
            P("kvh", "seq", None),
            P("seq"),
            P("seq", "kvh"),
            P("seq", "kvh"),
            P("kvh", "seq"),
        ),
        out_specs=P(None, ("seq", "kvh")),
        check_vma=False,
    )
```

```python
import functools

import jax
import jax.numpy as jnp
from jax import lax
from jax.experimental import pallas as pl
from jax.experimental.pallas import tpu as pltpu
from jax.sharding import Mesh, PartitionSpec as P

EPSILON = 1e-05
MASKED = -1e30
LANES = 128
CORES = 2
F32 = jnp.float32
BF16 = jnp.bfloat16


def dot(a, b):
    return jnp.dot(a, b, preferred_element_type=F32)


def split(array):
    high = array.astype(BF16)
    return high, (array - high.astype(F32)).astype(BF16)


def attend_kernel(batch, *refs):
    lengths_hbm, query_hbm, keys_hbm, values_hbm = refs[:4]
    ahead = (len(refs) - 10) // 2
    out = refs[4 + ahead]
    lengths, query, keys, values, sems = refs[-5:]
    later = [
        pltpu.make_async_copy(refs[4 + i], refs[5 + ahead + i], sems.at[2 + 2 * batch + i])
        for i in range(ahead)
    ]
    heads, head_dim = query.shape[1:]
    positions_here = keys.shape[1]
    loads = [
        pltpu.make_async_copy(lengths_hbm, lengths, sems.at[0]),
        pltpu.make_async_copy(query_hbm, query, sems.at[1]),
    ]
    key_loads, value_loads = [], []
    for b in range(batch):
        key_loads.append(pltpu.make_async_copy(keys_hbm.at[b], keys.at[b], sems.at[2 + 2 * b]))
        value_loads.append(pltpu.make_async_copy(values_hbm.at[b], values.at[b], sems.at[3 + 2 * b]))
    for load in loads:
        load.start()
    for b in range(batch):
        key_loads[b].start()
        value_loads[b].start()
    for load in later:
        load.start()
    for load in loads:
        load.wait()
    pieces = out.shape[0]
    per_head = pieces // heads
    width = head_dim // per_head
    stat = (LANES - width) // 2
    shard = lax.axis_index("chip") * CORES + lax.axis_index("core")
    positions = shard * positions_here + lax.broadcasted_iota(jnp.int32, (heads, positions_here), 1)
    for b in range(batch):
        key_loads[b].wait()
        scores = lax.dot_general(
            query[b], keys[b], (((1,), (1,)), ((), ())), preferred_element_type=F32
        ) * head_dim ** (-0.5)
        live = positions < lengths[b]
        masked = jnp.where(live, scores, MASKED)
        top = jnp.max(masked, axis=1, keepdims=True)
        weights = jnp.where(live, jnp.exp(masked - top), 0.0)
        total = jnp.sum(weights, axis=1, keepdims=True)
        value_loads[b].wait()
        both = dot(jnp.concatenate(split(weights), axis=0), values[b])
        sums = both[:heads] + both[heads:]
        stats = jnp.concatenate(
            [jnp.broadcast_to(top, (heads, stat)), jnp.broadcast_to(total, (heads, stat))], axis=1
        )
        for part in range(per_head):
            packed = jnp.concatenate([sums[:, part * width : (part + 1) * width], stats], axis=1)
            for h in range(heads):
                out[h * per_head + part, b : b + 1, :] = packed[h : h + 1]
    for load in later:
        load.wait()


def project_kernel(parts, weight, out):
    width = weight.shape[0]
    stat = (LANES - width) // 2
    got = parts[...]
    top = jnp.max(got[:, :, width : width + 1], axis=0)
    factor = jnp.exp(got[:, :, width : width + 1] - top[None])
    total = jnp.sum(factor * got[:, :, width + stat : width + stat + 1], axis=0)
    merged = jnp.sum(factor * got[:, :, :width], axis=0)
    attention = (merged / total).astype(BF16)
    tiles = out.shape[1] // attention.shape[0]
    columns = tiles * LANES
    for piece in range(out.shape[0]):
        term = dot(attention, weight[:, piece * columns : (piece + 1) * columns])
        out[piece] = jnp.concatenate(
            [term[:, tile * LANES : (tile + 1) * LANES] for tile in range(tiles)], axis=0
        ).astype(BF16)


def column_mask(shape, width):
    group = lax.axis_index("kvh")
    lanes = lax.broadcasted_iota(jnp.int32, shape, len(shape) - 1)
    return (lanes >= group * width) & (lanes < (group + 1) * width)


def carry_kernel(parts, residual, out):
    batch = residual.shape[0]
    stacked = jnp.sum(parts[...].astype(F32), axis=0)
    summed = jnp.concatenate(
        [stacked[row : row + batch] for row in range(0, stacked.shape[0], batch)], axis=1
    )
    spread = jnp.concatenate([residual[...]] * (summed.shape[1] // residual.shape[1]), axis=1)
    summed = summed + jnp.where(column_mask(summed.shape, residual.shape[1]), spread, 0.0)
    for piece in range(out.shape[0]):
        out[piece] = summed


def gate_kernel(parts, gain, gate_weight, up_weight, keep, give, carried_out):
    batch = parts.shape[1]
    carried = jnp.sum(parts[...], axis=0)
    width = carried_out.shape[1]
    own = jnp.where(column_mask(carried.shape, width), carried, 0.0)
    carried_out[...] = sum(
        own[:, piece * width : (piece + 1) * width] for piece in range(carried.shape[1] // width)
    )
    squares = jnp.sum(carried * carried, axis=1, keepdims=True)
    terms = jnp.concatenate(split(carried * gain[...]), axis=0)
    half = gate_weight.shape[1] // CORES
    first = lax.axis_index("core") == 0
    halves = []
    for core in range(CORES):
        lanes = slice(core * half, (core + 1) * half)
        gate = dot(terms, gate_weight[:, lanes])
        up = dot(terms, up_weight[:, lanes])
        halves.append(jnp.concatenate([gate[:batch] + gate[batch:], up[:batch] + up[batch:]], axis=0))
    keep[:, :half] = jnp.where(first, halves[0], halves[1])
    give[:, :half] = jnp.where(first, halves[1], halves[0])
    squares = jnp.broadcast_to(jnp.concatenate([squares, squares], axis=0), (2 * batch, LANES))
    keep[:, half:] = squares
    give[:, half:] = squares


def pair_kernel(keep, got, out):
    batch = keep.shape[0] // 2
    summed = keep[...] + got[...]
    half = summed.shape[1] - LANES
    high, low = split(summed[:batch, half:])
    packed = jnp.concatenate(
        [summed[:, :half].astype(BF16), jnp.concatenate([high, low], axis=0)], axis=1
    )
    middle = packed.shape[1] // 2
    packed = jnp.concatenate([packed[:, :middle], packed[:, middle:]], axis=0)
    for piece in range(out.shape[0]):
        out[piece] = packed


def activate_kernel(model_width, parts, out):
    batch = out.shape[0]
    stacked = jnp.sum(parts[...].astype(F32), axis=0)
    rows = stacked.shape[0] // 2
    summed = jnp.concatenate([stacked[:rows], stacked[rows:]], axis=1)
    half = out.shape[1]
    squares = summed[:batch, half : half + 1] + summed[batch:, half : half + 1]
    scale = lax.rsqrt(squares / model_width + EPSILON)
    gate = summed[:batch, :half] * scale
    up = summed[batch:, :half] * scale
    out[...] = (gate / (1.0 + jnp.exp(-gate)) * up).astype(BF16).astype(F32)


def down_kernel(own, other, weight, out):
    first = lax.axis_index("core") == 0
    half = own.shape[1]
    low = jnp.where(first, own[...], other[...]).astype(BF16)
    high = jnp.where(first, other[...], own[...]).astype(BF16)
    down = dot(low, weight[:half]) + dot(high, weight[half:])
    pieces = out.shape[0]
    width = down.shape[1] // pieces
    per_tile = LANES // width
    for piece in range(pieces):
        tile = down[:, piece // per_tile * LANES : (piece // per_tile + 1) * LANES]
        shift = piece % per_tile * width
        out[piece] = tile if shift == 0 else pltpu.roll(tile, LANES - shift, 1)


def finish_kernel(parts, carried, out):
    out[...] = carried[...] + jnp.sum(parts[...], axis=0)[:, : out.shape[1]]


VMEM = pl.BlockSpec(memory_space=pltpu.VMEM)
HBM = pl.BlockSpec(memory_space=pltpu.HBM)
WINDOW = pl.CostEstimate(flops=0, bytes_accessed=48 * 1024 * 1024, transcendentals=0)


def call(kernel, shapes, *args, specs=None, scratch=()):
    return pl.pallas_call(
        kernel,
        out_shape=shapes,
        in_specs=specs or [VMEM] * len(args),
        out_specs=jax.tree.map(lambda _: VMEM, shapes),
        scratch_shapes=scratch,
        cost_estimate=WINDOW,
        compiler_params=pltpu.CompilerParams(vmem_limit_bytes=16 * 1024 * 1024),
    )(*args)


def swap(array, axis):
    return lax.all_to_all(array, axis, split_axis=0, concat_axis=0, tiled=True)


def other_core(array):
    return lax.ppermute(array, "core", [(0, 1), (1, 0)])


def on_device(
    query,
    key_cache,
    value_cache,
    lengths,
    residual,
    out_weight,
    norm_gain,
    gate_weight,
    up_weight,
    down_weight,
):
    chips = lax.axis_size("chip")
    shards = chips * CORES
    groups = lax.axis_size("kvh")
    batch = query.shape[0]
    columns = norm_gain.shape[0]
    own = residual.shape[1]
    half = gate_weight.shape[1] // CORES
    padded = half + LANES

    def shape(*dims, dtype=F32):
        return jax.ShapeDtypeStruct(dims, dtype)

    keys = key_cache[:, :, 0, :]
    values = value_cache[:, :, 0, :]
    with jax.named_scope("attend"):
        ahead = (out_weight[0], up_weight, residual, norm_gain.reshape(1, columns))
        operands = [
            pltpu.with_memory_space_constraint(array, pltpu.HBM)
            for array in (lengths, query, keys, values, *ahead)
        ]
        partial, out_weight, up_weight, residual, gain = call(
            functools.partial(attend_kernel, batch),
            (
                shape(shards, batch, LANES),
                *(pltpu.VMEM(array.shape, array.dtype) for array in ahead),
            ),
            *operands,
            specs=[HBM] * len(operands),
            scratch=[
                pltpu.SMEM(lengths.shape, lengths.dtype),
                pltpu.VMEM(query.shape, query.dtype),
                pltpu.VMEM(keys.shape, keys.dtype),
                pltpu.VMEM(values.shape, values.dtype),
                pltpu.SemaphoreType.DMA((2 + 2 * batch + len(ahead),)),
            ],
        )
    partial = swap(partial, ("chip", "core"))
    with jax.named_scope("project"):
        projected = call(
            project_kernel,
            shape(shards, batch * columns // LANES, LANES, dtype=BF16),
            partial,
            out_weight,
        )
    projected = swap(projected, ("chip", "core"))
    with jax.named_scope("carry"):
        carried = call(carry_kernel, shape(groups, batch, columns), projected, residual)
    carried = swap(carried, "kvh")
    with jax.named_scope("gate_up"):
        keep, give, own_carried = call(
            gate_kernel,
            (shape(2 * batch, padded), shape(2 * batch, padded), shape(batch, own)),
            carried,
            gain,
            gate_weight,
            up_weight,
        )
    got = other_core(give)
    with jax.named_scope("pair"):
        hidden = call(pair_kernel, shape(chips, 4 * batch, padded // 2, dtype=BF16), keep, got)
    hidden = swap(hidden, "chip")
    with jax.named_scope("activate"):
        model_width = shards * columns
        activated = call(
            functools.partial(activate_kernel, model_width), shape(batch, half), hidden
        )
    other = other_core(activated)
    with jax.named_scope("down"):
        down = call(down_kernel, shape(groups, batch, LANES), activated, other, down_weight)
    down = swap(down, "kvh")
    with jax.named_scope("finish"):
        return call(finish_kernel, shape(batch, own), down, own_carried)


def solution(mesh):
    seq, kvh = mesh.devices.shape
    chips = Mesh(mesh.devices.reshape(seq // CORES, CORES, kvh), ("chip", "core", "kvh"))
    shard = ("chip", "core")
    return jax.shard_map(
        on_device,
        mesh=chips,
        in_specs=(
            P(None, "kvh", None),
            P(None, shard, "kvh", None),
            P(None, shard, "kvh", None),
            P(),
            P(None, (*shard, "kvh")),
            P("kvh", shard, None),
            P(shard),
            P(shard, "kvh"),
            P(shard, "kvh"),
            P("kvh", shard),
        ),
        out_specs=P(None, (*shard, "kvh")),
        check_vma=False,
    )
```

```python
import functools

import jax
import jax.numpy as jnp
from jax import lax
from jax.experimental import pallas as pl
from jax.experimental.pallas import tpu as pltpu
from jax.sharding import Mesh, PartitionSpec as P

EPSILON = 1e-05
MASKED = -1e30
LANES = 128
CORES = 2
F32 = jnp.float32
BF16 = jnp.bfloat16


def dot(a, b):
    return jnp.dot(a, b, preferred_element_type=F32)


def split(array):
    high = array.astype(BF16)
    return high, (array - high.astype(F32)).astype(BF16)


def attend_kernel(batch, *refs):
    lengths_hbm, query_hbm, keys_hbm, values_hbm = refs[:4]
    ahead = (len(refs) - 10) // 2
    out = refs[4 + ahead]
    lengths, query, keys, values, sems = refs[-5:]
    later = [
        pltpu.make_async_copy(refs[4 + i], refs[5 + ahead + i], sems.at[2 + 2 * batch + i])
        for i in range(ahead)
    ]
    heads, head_dim = query.shape[1:]
    positions_here = keys.shape[1]
    loads = [
        pltpu.make_async_copy(lengths_hbm, lengths, sems.at[0]),
        pltpu.make_async_copy(query_hbm, query, sems.at[1]),
    ]
    key_loads, value_loads = [], []
    for b in range(batch):
        key_loads.append(pltpu.make_async_copy(keys_hbm.at[b], keys.at[b], sems.at[2 + 2 * b]))
        value_loads.append(pltpu.make_async_copy(values_hbm.at[b], values.at[b], sems.at[3 + 2 * b]))
    for load in loads:
        load.start()
    for load in key_loads + value_loads + later:
        load.start()
    for load in loads:
        load.wait()
    pieces = out.shape[0]
    per_head = pieces // heads
    width = head_dim // per_head
    stat = (LANES - width) // 2
    shard = lax.axis_index("chip") * CORES + lax.axis_index("core")
    positions = shard * positions_here + lax.broadcasted_iota(jnp.int32, (heads, positions_here), 1)
    weights, tops, totals = [], [], []
    for load in key_loads:
        load.wait()
    for b in range(batch):
        scores = lax.dot_general(
            query[b], keys[b], (((1,), (1,)), ((), ())), preferred_element_type=F32
        ) * head_dim ** (-0.5)
        live = positions < lengths[b]
        masked = jnp.where(live, scores, MASKED)
        top = jnp.max(masked, axis=1, keepdims=True)
        weights.append(jnp.where(live, jnp.exp(masked - top), 0.0))
        tops.append(jnp.broadcast_to(top, (heads, stat)))
        totals.append(jnp.broadcast_to(jnp.sum(weights[b], axis=1, keepdims=True), (heads, stat)))
    for load in value_loads:
        load.wait()
    for b in range(batch):
        both = dot(jnp.concatenate(split(weights[b]), axis=0), values[b])
        sums = both[:heads] + both[heads:]
        for part in range(per_head):
            packed = jnp.concatenate(
                [sums[:, part * width : (part + 1) * width], tops[b], totals[b]], axis=1
            )
            for h in range(heads):
                out[h * per_head + part, b : b + 1, :] = packed[h : h + 1]
    for load in later:
        load.wait()


def project_kernel(parts, weight, *refs):
    out = refs[-1]
    width = weight.shape[0]
    stat = (LANES - width) // 2
    got = parts[...]
    top = jnp.max(got[:, :, width : width + 1], axis=0)
    factor = jnp.exp(got[:, :, width : width + 1] - top[None])
    total = jnp.sum(factor * got[:, :, width + stat : width + stat + 1], axis=0)
    merged = jnp.sum(factor * got[:, :, :width], axis=0)
    attention = (merged / total).astype(BF16)
    tiles = out.shape[1] // attention.shape[0]
    columns = tiles * LANES
    for piece in range(out.shape[0]):
        term = dot(attention, weight[:, piece * columns : (piece + 1) * columns])
        out[piece] = jnp.concatenate(
            [term[:, tile * LANES : (tile + 1) * LANES] for tile in range(tiles)], axis=0
        ).astype(BF16)


def column_mask(shape, width):
    group = lax.axis_index("kvh")
    lanes = lax.broadcasted_iota(jnp.int32, shape, len(shape) - 1)
    return (lanes >= group * width) & (lanes < (group + 1) * width)


def carry_kernel(parts, residual, out):
    batch = residual.shape[0]
    stacked = jnp.sum(parts[...].astype(F32), axis=0)
    summed = jnp.concatenate(
        [stacked[row : row + batch] for row in range(0, stacked.shape[0], batch)], axis=1
    )
    spread = jnp.concatenate([residual[...]] * (summed.shape[1] // residual.shape[1]), axis=1)
    summed = summed + jnp.where(column_mask(summed.shape, residual.shape[1]), spread, 0.0)
    for piece in range(out.shape[0]):
        out[piece] = summed


def gate_up_half(scaled, core, gate_weight, up_weight):
    batch = scaled.shape[0]
    terms = jnp.concatenate(split(scaled), axis=0)
    half = gate_weight.shape[1] // CORES
    lanes = pl.ds(pl.multiple_of(core * half, LANES), half)
    gate = dot(terms, gate_weight[:, lanes])
    up = dot(terms, up_weight[:, lanes])
    return jnp.concatenate([gate[:batch] + gate[batch:], up[:batch] + up[batch:]], axis=0)


def gate_give_kernel(parts, gain, gate_weight, up_weight, give, scaled_out, squares_out, carried_out):
    batch = parts.shape[1]
    carried = jnp.sum(parts[...], axis=0)
    width = carried_out.shape[1]
    own = jnp.where(column_mask(carried.shape, width), carried, 0.0)
    carried_out[...] = sum(
        own[:, piece * width : (piece + 1) * width] for piece in range(carried.shape[1] // width)
    )
    squares = jnp.sum(carried * carried, axis=1, keepdims=True)
    squares = jnp.broadcast_to(jnp.concatenate([squares, squares], axis=0), (2 * batch, LANES))
    scaled = carried * gain[...]
    half = gate_weight.shape[1] // CORES
    give[:, :half] = gate_up_half(scaled, 1 - lax.axis_index("core"), gate_weight, up_weight)
    give[:, half:] = squares
    scaled_out[...] = scaled
    squares_out[...] = squares


def gate_keep_kernel(scaled, squares, gate_weight, up_weight, keep):
    half = gate_weight.shape[1] // CORES
    keep[:, :half] = gate_up_half(scaled[...], lax.axis_index("core"), gate_weight, up_weight)
    keep[:, half:] = squares[...]


def pair_kernel(keep, got, out):
    batch = keep.shape[0] // 2
    summed = keep[...] + got[...]
    half = summed.shape[1] - LANES
    high, low = split(summed[:batch, half:])
    packed = jnp.concatenate(
        [summed[:, :half].astype(BF16), jnp.concatenate([high, low], axis=0)], axis=1
    )
    middle = packed.shape[1] // 2
    packed = jnp.concatenate([packed[:, :middle], packed[:, middle:]], axis=0)
    for piece in range(out.shape[0]):
        out[piece] = packed


def activate_kernel(model_width, parts, out):
    batch = out.shape[0]
    stacked = jnp.sum(parts[...].astype(F32), axis=0)
    rows = stacked.shape[0] // 2
    summed = jnp.concatenate([stacked[:rows], stacked[rows:]], axis=1)
    half = out.shape[1]
    squares = summed[:batch, half : half + 1] + summed[batch:, half : half + 1]
    scale = lax.rsqrt(squares / model_width + EPSILON)
    gate = summed[:batch, :half] * scale
    up = summed[batch:, :half] * scale
    out[...] = (gate / (1.0 + jnp.exp(-gate)) * up).astype(BF16).astype(F32)


def down_half(activated, core, weight):
    half = weight.shape[0] // CORES
    rows = pl.ds(pl.multiple_of(core * half, LANES), half)
    return dot(activated[...].astype(BF16), weight[rows, :])


def down_own_kernel(activated, weight, out):
    out[...] = down_half(activated, lax.axis_index("core"), weight)


def down_kernel(activated, weight, own, out):
    down = own[...] + down_half(activated, 1 - lax.axis_index("core"), weight)
    pieces = out.shape[0]
    width = down.shape[1] // pieces
    per_tile = LANES // width
    for piece in range(pieces):
        tile = down[:, piece // per_tile * LANES : (piece // per_tile + 1) * LANES]
        shift = piece % per_tile * width
        out[piece] = tile if shift == 0 else pltpu.roll(tile, LANES - shift, 1)


def finish_kernel(parts, carried, out):
    out[...] = carried[...] + jnp.sum(parts[...], axis=0)[:, : out.shape[1]]


VMEM = pl.BlockSpec(memory_space=pltpu.VMEM)
HBM = pl.BlockSpec(memory_space=pltpu.HBM)
SHORT = pl.CostEstimate(flops=0, bytes_accessed=2 * 1024 * 1024, transcendentals=0)


def call(kernel, shapes, *args, specs=None, scratch=()):
    return pl.pallas_call(
        kernel,
        out_shape=shapes,
        in_specs=specs or [VMEM] * len(args),
        out_specs=jax.tree.map(lambda _: VMEM, shapes),
        scratch_shapes=scratch,
        cost_estimate=SHORT,
        compiler_params=pltpu.CompilerParams(vmem_limit_bytes=16 * 1024 * 1024),
    )(*args)


def swap(array, axis):
    return lax.all_to_all(array, axis, split_axis=0, concat_axis=0, tiled=True)


def other_core(array):
    return lax.ppermute(array, "core", [(0, 1), (1, 0)])


def on_device(
    query,
    key_cache,
    value_cache,
    lengths,
    residual,
    out_weight,
    norm_gain,
    gate_weight,
    up_weight,
    down_weight,
):
    chips = lax.axis_size("chip")
    shards = chips * CORES
    groups = lax.axis_size("kvh")
    batch = query.shape[0]
    columns = norm_gain.shape[0]
    own = residual.shape[1]
    half = gate_weight.shape[1] // CORES
    padded = half + LANES

    def shape(*dims, dtype=F32):
        return jax.ShapeDtypeStruct(dims, dtype)

    keys = key_cache[:, :, 0, :]
    values = value_cache[:, :, 0, :]
    with jax.named_scope("attend"):
        ahead = (out_weight[0], residual, norm_gain.reshape(1, columns))
        operands = [
            pltpu.with_memory_space_constraint(array, pltpu.HBM)
            for array in (lengths, query, keys, values, *ahead)
        ]
        partial, out_weight, residual, gain = call(
            functools.partial(attend_kernel, batch),
            (
                shape(shards, batch, LANES),
                *(pltpu.VMEM(array.shape, array.dtype) for array in ahead),
            ),
            *operands,
            specs=[HBM] * len(operands),
            scratch=[
                pltpu.SMEM(lengths.shape, lengths.dtype),
                pltpu.VMEM(query.shape, query.dtype),
                pltpu.VMEM(keys.shape, keys.dtype),
                pltpu.VMEM(values.shape, values.dtype),
                pltpu.SemaphoreType.DMA((2 + 2 * batch + len(ahead),)),
            ],
        )
    partial = swap(partial, ("chip", "core"))
    with jax.named_scope("project"):
        projected = call(
            project_kernel,
            shape(shards, batch * columns // LANES, LANES, dtype=BF16),
            partial,
            out_weight,
            *(
                pltpu.with_memory_space_constraint(array, pltpu.HBM)
                for array in (gate_weight, up_weight, down_weight)
            ),
            specs=[VMEM] * 2 + [HBM] * 3,
        )
    projected = swap(projected, ("chip", "core"))
    with jax.named_scope("carry"):
        carried = call(carry_kernel, shape(groups, batch, columns), projected, residual)
    carried = swap(carried, "kvh")
    with jax.named_scope("gate_up_give"):
        give, scaled, squares, own_carried = call(
            gate_give_kernel,
            (
                shape(2 * batch, padded),
                shape(batch, columns),
                shape(2 * batch, LANES),
                shape(batch, own),
            ),
            carried,
            gain,
            gate_weight,
            up_weight,
        )
    got = other_core(give)
    with jax.named_scope("gate_up_keep"):
        keep = call(
            gate_keep_kernel, shape(2 * batch, padded), scaled, squares, gate_weight, up_weight
        )
    with jax.named_scope("pair"):
        hidden = call(pair_kernel, shape(chips, 4 * batch, padded // 2, dtype=BF16), keep, got)
    hidden = swap(hidden, "chip")
    with jax.named_scope("activate"):
        model_width = shards * columns
        activated = call(
            functools.partial(activate_kernel, model_width), shape(batch, half), hidden
        )
    other = other_core(activated)
    with jax.named_scope("down_own"):
        down = call(down_own_kernel, shape(batch, columns), activated, down_weight)
    with jax.named_scope("down"):
        down = call(down_kernel, shape(groups, batch, LANES), other, down_weight, down)
    down = swap(down, "kvh")
    with jax.named_scope("finish"):
        return call(finish_kernel, shape(batch, own), down, own_carried)


def solution(mesh):
    seq, kvh = mesh.devices.shape
    chips = Mesh(mesh.devices.reshape(seq // CORES, CORES, kvh), ("chip", "core", "kvh"))
    shard = ("chip", "core")
    return jax.shard_map(
        on_device,
        mesh=chips,
        in_specs=(
            P(None, "kvh", None),
            P(None, shard, "kvh", None),
            P(None, shard, "kvh", None),
            P(),
            P(None, (*shard, "kvh")),
            P("kvh", shard, None),
            P(shard),
            P(shard, "kvh"),
            P(shard, "kvh"),
            P("kvh", shard),
        ),
        out_specs=P(None, (*shard, "kvh")),
        check_vma=False,
    )
```

```python
import functools

import jax
import jax.numpy as jnp
from jax import lax
from jax.experimental import pallas as pl
from jax.experimental.pallas import tpu as pltpu
from jax.sharding import Mesh, PartitionSpec as P

EPSILON = 1e-05
MASKED = -1e30
LANES = 128
CORES = 2
F32 = jnp.float32
BF16 = jnp.bfloat16


def dot(a, b):
    return jnp.dot(a, b, preferred_element_type=F32)


def split(array):
    high = array.astype(BF16)
    return high, (array - high.astype(F32)).astype(BF16)


def attend_kernel(batch, *refs):
    lengths_hbm, query_hbm, keys_hbm, values_hbm = refs[:4]
    ahead = (len(refs) - 14) // 2
    out = refs[8 + ahead]
    lengths, query, keys, values, sems = refs[-5:]
    later = [
        pltpu.make_async_copy(refs[4 + i], refs[9 + ahead + i], sems.at[4 + i])
        for i in range(ahead)
    ]
    heads, head_dim = query.shape[1:]
    positions_here = keys.shape[1]
    loads = [
        pltpu.make_async_copy(lengths_hbm, lengths, sems.at[0]),
        pltpu.make_async_copy(query_hbm, query, sems.at[1]),
    ]
    key_load = pltpu.make_async_copy(keys_hbm, keys, sems.at[2])
    value_load = pltpu.make_async_copy(values_hbm, values, sems.at[3])
    for load in (*loads, key_load, value_load, *later):
        load.start()
    for load in loads:
        load.wait()
    pieces = out.shape[0]
    per_head = pieces // heads
    width = head_dim // per_head
    stat = (LANES - width) // 2
    shard = lax.axis_index("chip") * CORES + lax.axis_index("core")
    positions = shard * positions_here + lax.broadcasted_iota(jnp.int32, (heads, positions_here), 1)
    weights, tops, totals = [], [], []
    key_load.wait()
    for b in range(batch):
        scores = lax.dot_general(
            query[b], keys[b], (((1,), (1,)), ((), ())), preferred_element_type=F32
        ) * head_dim ** (-0.5)
        live = positions < lengths[b]
        masked = jnp.where(live, scores, MASKED)
        top = jnp.max(masked, axis=1, keepdims=True)
        weights.append(jnp.where(live, jnp.exp(masked - top), 0.0))
        tops.append(jnp.broadcast_to(top, (heads, stat)))
        totals.append(jnp.broadcast_to(jnp.sum(weights[b], axis=1, keepdims=True), (heads, stat)))
    value_load.wait()
    for b in range(batch):
        both = dot(jnp.concatenate(split(weights[b]), axis=0), values[b])
        sums = both[:heads] + both[heads:]
        for part in range(per_head):
            packed = jnp.concatenate(
                [sums[:, part * width : (part + 1) * width], tops[b], totals[b]], axis=1
            )
            for h in range(heads):
                out[h * per_head + part, b : b + 1, :] = packed[h : h + 1]
    for load in later:
        load.wait()


def project_kernel(parts, weight, out):
    width = weight.shape[0]
    stat = (LANES - width) // 2
    got = parts[...]
    top = jnp.max(got[:, :, width : width + 1], axis=0)
    factor = jnp.exp(got[:, :, width : width + 1] - top[None])
    total = jnp.sum(factor * got[:, :, width + stat : width + stat + 1], axis=0)
    merged = jnp.sum(factor * got[:, :, :width], axis=0)
    attention = (merged / total).astype(BF16)
    tiles = out.shape[1] // attention.shape[0]
    columns = tiles * LANES
    for piece in range(out.shape[0]):
        term = dot(attention, weight[:, piece * columns : (piece + 1) * columns])
        out[piece] = jnp.concatenate(
            [term[:, tile * LANES : (tile + 1) * LANES] for tile in range(tiles)], axis=0
        ).astype(BF16)


def column_mask(shape, width):
    group = lax.axis_index("kvh")
    lanes = lax.broadcasted_iota(jnp.int32, shape, len(shape) - 1)
    return (lanes >= group * width) & (lanes < (group + 1) * width)


def carry_kernel(parts, residual, out):
    batch = residual.shape[0]
    stacked = jnp.sum(parts[...].astype(F32), axis=0)
    summed = jnp.concatenate(
        [stacked[row : row + batch] for row in range(0, stacked.shape[0], batch)], axis=1
    )
    spread = jnp.concatenate([residual[...]] * (summed.shape[1] // residual.shape[1]), axis=1)
    summed = summed + jnp.where(column_mask(summed.shape, residual.shape[1]), spread, 0.0)
    for piece in range(out.shape[0]):
        out[piece] = summed


def gate_up_half(scaled, core, gate_weight, up_weight):
    batch = scaled.shape[0]
    terms = jnp.concatenate(split(scaled), axis=0)
    half = gate_weight.shape[1] // CORES
    lanes = pl.ds(pl.multiple_of(core * half, LANES), half)
    gate = dot(terms, gate_weight[:, lanes])
    up = dot(terms, up_weight[:, lanes])
    return jnp.concatenate([gate[:batch] + gate[batch:], up[:batch] + up[batch:]], axis=0)


def gate_give_kernel(
    parts, gain, gate_weight, up_weight, _, give, scaled_out, squares_out, carried_out
):
    batch = parts.shape[1]
    carried = jnp.sum(parts[...], axis=0)
    width = carried_out.shape[1]
    own = jnp.where(column_mask(carried.shape, width), carried, 0.0)
    carried_out[...] = sum(
        own[:, piece * width : (piece + 1) * width] for piece in range(carried.shape[1] // width)
    )
    squares = jnp.sum(carried * carried, axis=1, keepdims=True)
    squares = jnp.broadcast_to(jnp.concatenate([squares, squares], axis=0), (2 * batch, LANES))
    scaled = carried * gain[...]
    half = gate_weight.shape[1] // CORES
    give[:, :half] = gate_up_half(scaled, 1 - lax.axis_index("core"), gate_weight, up_weight)
    give[:, half:] = squares
    scaled_out[...] = scaled
    squares_out[...] = squares


def gate_keep_kernel(scaled, squares, gate_weight, up_weight, keep):
    half = gate_weight.shape[1] // CORES
    keep[:, :half] = gate_up_half(scaled[...], lax.axis_index("core"), gate_weight, up_weight)
    keep[:, half:] = squares[...]


def pair_kernel(keep, got, out):
    batch = keep.shape[0] // 2
    summed = keep[...] + got[...]
    half = summed.shape[1] - LANES
    high, low = split(summed[:batch, half:])
    packed = jnp.concatenate(
        [summed[:, :half].astype(BF16), jnp.concatenate([high, low], axis=0)], axis=1
    )
    middle = packed.shape[1] // 2
    packed = jnp.concatenate([packed[:, :middle], packed[:, middle:]], axis=0)
    for piece in range(out.shape[0]):
        out[piece] = packed


def activate_kernel(model_width, parts, out):
    batch = out.shape[0]
    stacked = jnp.sum(parts[...].astype(F32), axis=0)
    rows = stacked.shape[0] // 2
    summed = jnp.concatenate([stacked[:rows], stacked[rows:]], axis=1)
    half = out.shape[1]
    squares = summed[:batch, half : half + 1] + summed[batch:, half : half + 1]
    scale = lax.rsqrt(squares / model_width + EPSILON)
    gate = summed[:batch, :half] * scale
    up = summed[batch:, :half] * scale
    out[...] = (gate / (1.0 + jnp.exp(-gate)) * up).astype(BF16).astype(F32)


def down_half(activated, core, weight):
    half = weight.shape[0] // CORES
    rows = pl.ds(pl.multiple_of(core * half, LANES), half)
    return dot(activated[...].astype(BF16), weight[rows, :])


def down_own_kernel(activated, weight, out):
    out[...] = down_half(activated, lax.axis_index("core"), weight)


def down_kernel(activated, weight, own, out):
    down = own[...] + down_half(activated, 1 - lax.axis_index("core"), weight)
    pieces = out.shape[0]
    width = down.shape[1] // pieces
    per_tile = LANES // width
    for piece in range(pieces):
        tile = down[:, piece // per_tile * LANES : (piece // per_tile + 1) * LANES]
        shift = piece % per_tile * width
        out[piece] = tile if shift == 0 else pltpu.roll(tile, LANES - shift, 1)


def finish_kernel(parts, carried, out):
    out[...] = carried[...] + jnp.sum(parts[...], axis=0)[:, : out.shape[1]]


VMEM = pl.BlockSpec(memory_space=pltpu.VMEM)
HBM = pl.BlockSpec(memory_space=pltpu.HBM)
SHORT = pl.CostEstimate(flops=0, bytes_accessed=2 * 1024 * 1024, transcendentals=0)


def call(kernel, shapes, *args, specs=None, scratch=()):
    return pl.pallas_call(
        kernel,
        out_shape=shapes,
        in_specs=specs or [VMEM] * len(args),
        out_specs=jax.tree.map(lambda _: VMEM, shapes),
        scratch_shapes=scratch,
        cost_estimate=SHORT,
        compiler_params=pltpu.CompilerParams(vmem_limit_bytes=16 * 1024 * 1024),
    )(*args)


def swap(array, axis):
    return lax.all_to_all(array, axis, split_axis=0, concat_axis=0, tiled=True)


def other_core(array):
    return lax.ppermute(array, "core", [(0, 1), (1, 0)])


def on_device(
    query,
    key_cache,
    value_cache,
    lengths,
    residual,
    out_weight,
    norm_gain,
    gate_weight,
    up_weight,
    down_weight,
):
    chips = lax.axis_size("chip")
    shards = chips * CORES
    groups = lax.axis_size("kvh")
    batch = query.shape[0]
    columns = norm_gain.shape[0]
    own = residual.shape[1]
    half = gate_weight.shape[1] // CORES
    padded = half + LANES

    def shape(*dims, dtype=F32):
        return jax.ShapeDtypeStruct(dims, dtype)

    keys = key_cache[:, :, 0, :]
    values = value_cache[:, :, 0, :]
    with jax.named_scope("attend"):
        ahead = (residual, norm_gain.reshape(1, columns))
        operands = [
            pltpu.with_memory_space_constraint(array, pltpu.HBM)
            for array in (lengths, query, keys, values, *ahead, out_weight, gate_weight, up_weight, down_weight)
        ]
        partial, residual, gain = call(
            functools.partial(attend_kernel, batch),
            (
                shape(shards, batch, LANES),
                *(pltpu.VMEM(array.shape, array.dtype) for array in ahead),
            ),
            *operands,
            specs=[HBM] * len(operands),
            scratch=[
                pltpu.SMEM(lengths.shape, lengths.dtype),
                pltpu.VMEM(query.shape, query.dtype),
                pltpu.VMEM(keys.shape, keys.dtype),
                pltpu.VMEM(values.shape, values.dtype),
                pltpu.SemaphoreType.DMA((4 + len(ahead),)),
            ],
        )
    partial = swap(partial, ("chip", "core"))
    with jax.named_scope("project"):
        projected = call(
            project_kernel,
            shape(shards, batch * columns // LANES, LANES, dtype=BF16),
            partial,
            out_weight[0],
        )
    projected = swap(projected, ("chip", "core"))
    with jax.named_scope("carry"):
        carried = call(carry_kernel, shape(groups, batch, columns), projected, residual)
    carried = swap(carried, "kvh")
    with jax.named_scope("gate_up_give"):
        give, scaled, squares, own_carried = call(
            gate_give_kernel,
            (
                shape(2 * batch, padded),
                shape(batch, columns),
                shape(2 * batch, LANES),
                shape(batch, own),
            ),
            carried,
            gain,
            gate_weight,
            up_weight,
            down_weight,
        )
    got = other_core(give)
    with jax.named_scope("gate_up_keep"):
        keep = call(
            gate_keep_kernel, shape(2 * batch, padded), scaled, squares, gate_weight, up_weight
        )
    with jax.named_scope("pair"):
        hidden = call(pair_kernel, shape(chips, 4 * batch, padded // 2, dtype=BF16), keep, got)
    hidden = swap(hidden, "chip")
    with jax.named_scope("activate"):
        model_width = shards * columns
        activated = call(
            functools.partial(activate_kernel, model_width), shape(batch, half), hidden
        )
    other = other_core(activated)
    with jax.named_scope("down_own"):
        down = call(down_own_kernel, shape(batch, columns), activated, down_weight)
    with jax.named_scope("down"):
        down = call(down_kernel, shape(groups, batch, LANES), other, down_weight, down)
    down = swap(down, "kvh")
    with jax.named_scope("finish"):
        return call(finish_kernel, shape(batch, own), down, own_carried)


def solution(mesh):
    seq, kvh = mesh.devices.shape
    chips = Mesh(mesh.devices.reshape(seq // CORES, CORES, kvh), ("chip", "core", "kvh"))
    shard = ("chip", "core")
    return jax.shard_map(
        on_device,
        mesh=chips,
        in_specs=(
            P(None, "kvh", None),
            P(None, shard, "kvh", None),
            P(None, shard, "kvh", None),
            P(),
            P(None, (*shard, "kvh")),
            P("kvh", shard, None),
            P(shard),
            P(shard, "kvh"),
            P(shard, "kvh"),
            P("kvh", shard),
        ),
        out_specs=P(None, (*shard, "kvh")),
        check_vma=False,
    )
```

```python
import functools

import jax
import jax.numpy as jnp
from jax import lax
from jax.experimental import pallas as pl
from jax.experimental.pallas import tpu as pltpu
from jax.sharding import Mesh, PartitionSpec as P

EPSILON = 1e-05
MASKED = -1e30
LANES = 128
CORES = 2
F32 = jnp.float32
BF16 = jnp.bfloat16


def dot(a, b):
    return jnp.dot(a, b, preferred_element_type=F32)


def split(array):
    high = array.astype(BF16)
    return high, (array - high.astype(F32)).astype(BF16)


def attend_kernel(batch, *refs):
    lengths_hbm, query_hbm, keys_hbm, values_hbm = refs[:4]
    ahead = (len(refs) - 14) // 2
    out = refs[8 + ahead]
    lengths, query, keys, values, sems = refs[-5:]
    later = [
        pltpu.make_async_copy(refs[4 + i], refs[9 + ahead + i], sems.at[4 + i])
        for i in range(ahead)
    ]
    heads, head_dim = query.shape[1:]
    positions_here = keys.shape[1]
    loads = [
        pltpu.make_async_copy(lengths_hbm, lengths, sems.at[0]),
        pltpu.make_async_copy(query_hbm, query, sems.at[1]),
    ]
    key_load = pltpu.make_async_copy(keys_hbm, keys, sems.at[2])
    value_load = pltpu.make_async_copy(values_hbm, values, sems.at[3])
    for load in (*loads, key_load, value_load, *later):
        load.start()
    for load in loads:
        load.wait()
    pieces = out.shape[0]
    per_head = pieces // heads
    width = head_dim // per_head
    stat = (LANES - width) // 2
    shard = lax.axis_index("chip") * CORES + lax.axis_index("core")
    positions = shard * positions_here + lax.broadcasted_iota(jnp.int32, (heads, positions_here), 1)
    weights, tops, totals = [], [], []
    key_load.wait()
    for b in range(batch):
        scores = lax.dot_general(
            query[b], keys[b], (((1,), (1,)), ((), ())), preferred_element_type=F32
        ) * head_dim ** (-0.5)
        live = positions < lengths[b]
        masked = jnp.where(live, scores, MASKED)
        top = jnp.max(masked, axis=1, keepdims=True)
        weights.append(jnp.where(live, jnp.exp(masked - top), 0.0))
        tops.append(jnp.broadcast_to(top, (heads, stat)))
        totals.append(jnp.broadcast_to(jnp.sum(weights[b], axis=1, keepdims=True), (heads, stat)))
    value_load.wait()
    for b in range(batch):
        both = dot(jnp.concatenate(split(weights[b]), axis=0), values[b])
        sums = both[:heads] + both[heads:]
        for part in range(per_head):
            packed = jnp.concatenate(
                [sums[:, part * width : (part + 1) * width], tops[b], totals[b]], axis=1
            )
            for h in range(heads):
                out[h * per_head + part, b : b + 1, :] = packed[h : h + 1]
    for load in later:
        load.wait()


def project_kernel(parts, weight, out):
    width = weight.shape[0]
    stat = (LANES - width) // 2
    got = parts[...]
    top = jnp.max(got[:, :, width : width + 1], axis=0)
    factor = jnp.exp(got[:, :, width : width + 1] - top[None])
    total = jnp.sum(factor * got[:, :, width + stat : width + stat + 1], axis=0)
    merged = jnp.sum(factor * got[:, :, :width], axis=0)
    attention = (merged / total).astype(BF16)
    tiles = out.shape[1] // attention.shape[0]
    columns = tiles * LANES
    for piece in range(out.shape[0]):
        term = dot(attention, weight[:, piece * columns : (piece + 1) * columns])
        out[piece] = jnp.concatenate(
            [term[:, tile * LANES : (tile + 1) * LANES] for tile in range(tiles)], axis=0
        ).astype(BF16)


def column_mask(shape, width):
    group = lax.axis_index("kvh")
    lanes = lax.broadcasted_iota(jnp.int32, shape, len(shape) - 1)
    return (lanes >= group * width) & (lanes < (group + 1) * width)


def carry_kernel(parts, residual, out):
    batch = residual.shape[0]
    stacked = jnp.sum(parts[...].astype(F32), axis=0)
    summed = jnp.concatenate(
        [stacked[row : row + batch] for row in range(0, stacked.shape[0], batch)], axis=1
    )
    spread = jnp.concatenate([residual[...]] * (summed.shape[1] // residual.shape[1]), axis=1)
    summed = summed + jnp.where(column_mask(summed.shape, residual.shape[1]), spread, 0.0)
    for piece in range(out.shape[0]):
        out[piece] = summed


def gate_up_half(scaled, core, gate_weight, up_weight):
    batch = scaled.shape[0]
    terms = jnp.concatenate(split(scaled), axis=0)
    half = gate_weight.shape[1] // CORES
    lanes = pl.ds(pl.multiple_of(core * half, LANES), half)
    gate = dot(terms, gate_weight[:, lanes])
    up = dot(terms, up_weight[:, lanes])
    return jnp.concatenate([gate[:batch] + gate[batch:], up[:batch] + up[batch:]], axis=0)


def gate_give_kernel(
    parts, gain, gate_weight, up_weight, _, give, scaled_out, squares_out, carried_out
):
    batch = parts.shape[1]
    carried = jnp.sum(parts[...], axis=0)
    width = carried_out.shape[1]
    own = jnp.where(column_mask(carried.shape, width), carried, 0.0)
    carried_out[...] = sum(
        own[:, piece * width : (piece + 1) * width] for piece in range(carried.shape[1] // width)
    )
    squares = jnp.sum(carried * carried, axis=1, keepdims=True)
    squares = jnp.broadcast_to(jnp.concatenate([squares, squares], axis=0), (2 * batch, LANES))
    scaled = carried * gain[...]
    half = gate_weight.shape[1] // CORES
    give[:, :half] = gate_up_half(scaled, 1 - lax.axis_index("core"), gate_weight, up_weight)
    give[:, half:] = squares
    scaled_out[...] = scaled
    squares_out[...] = squares


def gate_keep_kernel(scaled, squares, gate_weight, up_weight, keep):
    half = gate_weight.shape[1] // CORES
    keep[:, :half] = gate_up_half(scaled[...], lax.axis_index("core"), gate_weight, up_weight)
    keep[:, half:] = squares[...]


def pair_kernel(keep, got, out):
    batch = keep.shape[0] // 2
    summed = keep[...] + got[...]
    half = summed.shape[1] - LANES
    terms, squares = summed[:, :half], summed[:, half:]

    def exponent(top):
        return jnp.ceil(jnp.log2(jnp.maximum(top, 1e-30)))

    rows = exponent(jnp.max(jnp.abs(terms), axis=1, keepdims=True))
    sums = exponent(squares)
    high, low = split(squares * jnp.exp2(-sums))
    lane = lax.broadcasted_iota(jnp.int32, squares.shape, 1)
    extra = jnp.where(
        lane < LANES // 4,
        rows,
        jnp.where(
            lane < LANES // 2,
            sums,
            jnp.where(lane < 3 * LANES // 4, high.astype(F32), low.astype(F32)),
        ),
    )
    packed = jnp.concatenate([terms * jnp.exp2(-rows), extra], axis=1)
    middle = packed.shape[1] // 2
    out[...] = jnp.concatenate([packed[:, :middle], packed[:, middle:]], axis=0)


def activate_kernel(model_width, parts, out):
    batch = out.shape[0]
    half = out.shape[1]
    terms, squares = 0.0, 0.0
    for chip in range(parts.shape[0]):
        rows = parts.shape[1] // 2
        part = jnp.concatenate([parts[chip, :rows], parts[chip, rows:]], axis=1)
        extra = part[:, half:]
        terms = terms + part[:, :half] * jnp.exp2(extra[:, :1])
        quarter = LANES // 4
        squares = squares + jnp.exp2(extra[:, quarter : quarter + 1]) * (
            extra[:, 2 * quarter : 2 * quarter + 1] + extra[:, 3 * quarter : 3 * quarter + 1]
        )
    scale = lax.rsqrt(squares / model_width + EPSILON)
    terms = terms * scale
    gate, up = terms[:batch], terms[batch:]
    out[...] = (gate / (1.0 + jnp.exp(-gate)) * up).astype(BF16).astype(F32)


def down_half(activated, core, weight):
    half = weight.shape[0] // CORES
    rows = pl.ds(pl.multiple_of(core * half, LANES), half)
    return dot(activated[...].astype(BF16), weight[rows, :])


def down_own_kernel(activated, weight, out):
    out[...] = down_half(activated, lax.axis_index("core"), weight)


def down_kernel(activated, weight, own, out):
    down = own[...] + down_half(activated, 1 - lax.axis_index("core"), weight)
    pieces = out.shape[0]
    width = down.shape[1] // pieces
    per_tile = LANES // width
    for piece in range(pieces):
        tile = down[:, piece // per_tile * LANES : (piece // per_tile + 1) * LANES]
        shift = piece % per_tile * width
        out[piece] = tile if shift == 0 else pltpu.roll(tile, LANES - shift, 1)


def finish_kernel(parts, carried, out):
    out[...] = carried[...] + jnp.sum(parts[...], axis=0)[:, : out.shape[1]]


VMEM = pl.BlockSpec(memory_space=pltpu.VMEM)
HBM = pl.BlockSpec(memory_space=pltpu.HBM)
SHORT = pl.CostEstimate(flops=0, bytes_accessed=2 * 1024 * 1024, transcendentals=0)


def call(kernel, shapes, *args, specs=None, scratch=()):
    return pl.pallas_call(
        kernel,
        out_shape=shapes,
        in_specs=specs or [VMEM] * len(args),
        out_specs=jax.tree.map(lambda _: VMEM, shapes),
        scratch_shapes=scratch,
        cost_estimate=SHORT,
        compiler_params=pltpu.CompilerParams(vmem_limit_bytes=16 * 1024 * 1024),
    )(*args)


def swap(array, axis):
    return lax.all_to_all(array, axis, split_axis=0, concat_axis=0, tiled=True)


def other_core(array):
    return lax.ppermute(array, "core", [(0, 1), (1, 0)])


def on_device(
    query,
    key_cache,
    value_cache,
    lengths,
    residual,
    out_weight,
    norm_gain,
    gate_weight,
    up_weight,
    down_weight,
):
    chips = lax.axis_size("chip")
    shards = chips * CORES
    groups = lax.axis_size("kvh")
    batch = query.shape[0]
    columns = norm_gain.shape[0]
    own = residual.shape[1]
    half = gate_weight.shape[1] // CORES
    padded = half + LANES

    def shape(*dims, dtype=F32):
        return jax.ShapeDtypeStruct(dims, dtype)

    keys = key_cache[:, :, 0, :]
    values = value_cache[:, :, 0, :]
    with jax.named_scope("attend"):
        ahead = (residual, norm_gain.reshape(1, columns))
        operands = [
            pltpu.with_memory_space_constraint(array, pltpu.HBM)
            for array in (lengths, query, keys, values, *ahead, out_weight, gate_weight, up_weight, down_weight)
        ]
        partial, residual, gain = call(
            functools.partial(attend_kernel, batch),
            (
                shape(shards, batch, LANES),
                *(pltpu.VMEM(array.shape, array.dtype) for array in ahead),
            ),
            *operands,
            specs=[HBM] * len(operands),
            scratch=[
                pltpu.SMEM(lengths.shape, lengths.dtype),
                pltpu.VMEM(query.shape, query.dtype),
                pltpu.VMEM(keys.shape, keys.dtype),
                pltpu.VMEM(values.shape, values.dtype),
                pltpu.SemaphoreType.DMA((4 + len(ahead),)),
            ],
        )
    partial = swap(partial, ("chip", "core"))
    with jax.named_scope("project"):
        projected = call(
            project_kernel,
            shape(shards, batch * columns // LANES, LANES, dtype=BF16),
            partial,
            out_weight[0],
        )
    projected = swap(projected, ("chip", "core"))
    with jax.named_scope("carry"):
        carried = call(carry_kernel, shape(groups, batch, columns), projected, residual)
    carried = swap(carried, "kvh")
    with jax.named_scope("gate_up_give"):
        give, scaled, squares, own_carried = call(
            gate_give_kernel,
            (
                shape(2 * batch, padded),
                shape(batch, columns),
                shape(2 * batch, LANES),
                shape(batch, own),
            ),
            carried,
            gain,
            gate_weight,
            up_weight,
            down_weight,
        )
    got = other_core(give)
    with jax.named_scope("gate_up_keep"):
        keep = call(
            gate_keep_kernel, shape(2 * batch, padded), scaled, squares, gate_weight, up_weight
        )
    with jax.named_scope("pair"):
        hidden = call(pair_kernel, shape(4 * batch, padded // 2), keep, got)
    hidden = jnp.broadcast_to(hidden.astype(jnp.float16)[None], (chips, *hidden.shape))
    hidden = swap(hidden, "chip").astype(F32)
    with jax.named_scope("activate"):
        model_width = shards * columns
        activated = call(
            functools.partial(activate_kernel, model_width), shape(batch, half), hidden
        )
    other = other_core(activated)
    with jax.named_scope("down_own"):
        down = call(down_own_kernel, shape(batch, columns), activated, down_weight)
    with jax.named_scope("down"):
        down = call(down_kernel, shape(groups, batch, LANES), other, down_weight, down)
    down = swap(down, "kvh")
    with jax.named_scope("finish"):
        return call(finish_kernel, shape(batch, own), down, own_carried)


def solution(mesh):
    seq, kvh = mesh.devices.shape
    chips = Mesh(mesh.devices.reshape(seq // CORES, CORES, kvh), ("chip", "core", "kvh"))
    shard = ("chip", "core")
    return jax.shard_map(
        on_device,
        mesh=chips,
        in_specs=(
            P(None, "kvh", None),
            P(None, shard, "kvh", None),
            P(None, shard, "kvh", None),
            P(),
            P(None, (*shard, "kvh")),
            P("kvh", shard, None),
            P(shard),
            P(shard, "kvh"),
            P(shard, "kvh"),
            P("kvh", shard),
        ),
        out_specs=P(None, (*shard, "kvh")),
        check_vma=False,
    )
```

```python
import functools

import jax
import jax.numpy as jnp
from jax import lax
from jax.experimental import pallas as pl
from jax.experimental.pallas import tpu as pltpu
from jax.sharding import Mesh, PartitionSpec as P

EPSILON = 1e-05
MASKED = -1e30
LANES = 128
CORES = 2
F32 = jnp.float32
BF16 = jnp.bfloat16


def dot(a, b):
    return jnp.dot(a, b, preferred_element_type=F32)


def split(array):
    high = array.astype(BF16)
    return high, (array - high.astype(F32)).astype(BF16)


def attend_kernel(batch, *refs):
    lengths_hbm, query_hbm, keys_hbm, values_hbm = refs[:4]
    ahead = (len(refs) - 14) // 2
    out = refs[8 + ahead]
    lengths, query, keys, values, sems = refs[-5:]
    later = [
        pltpu.make_async_copy(refs[4 + i], refs[9 + ahead + i], sems.at[4 + i])
        for i in range(ahead)
    ]
    heads, head_dim = query.shape[1:]
    positions_here = keys.shape[1]
    loads = [
        pltpu.make_async_copy(lengths_hbm, lengths, sems.at[0]),
        pltpu.make_async_copy(query_hbm, query, sems.at[1]),
    ]
    key_load = pltpu.make_async_copy(keys_hbm, keys, sems.at[2])
    value_load = pltpu.make_async_copy(values_hbm, values, sems.at[3])
    for load in (*loads, key_load, value_load, *later):
        load.start()
    for load in loads:
        load.wait()
    pieces = out.shape[0]
    per_head = pieces // heads
    width = head_dim // per_head
    stat = (LANES - width) // 2
    shard = lax.axis_index("chip") * CORES + lax.axis_index("core")
    positions = shard * positions_here + lax.broadcasted_iota(jnp.int32, (heads, positions_here), 1)
    weights, tops, totals = [], [], []
    key_load.wait()
    for b in range(batch):
        scores = lax.dot_general(
            query[b], keys[b], (((1,), (1,)), ((), ())), preferred_element_type=F32
        ) * head_dim ** (-0.5)
        live = positions < lengths[b]
        masked = jnp.where(live, scores, MASKED)
        top = jnp.max(masked, axis=1, keepdims=True)
        weights.append(jnp.where(live, jnp.exp(masked - top), 0.0))
        tops.append(jnp.broadcast_to(top, (heads, stat)))
        totals.append(jnp.broadcast_to(jnp.sum(weights[b], axis=1, keepdims=True), (heads, stat)))
    value_load.wait()
    for b in range(batch):
        both = dot(jnp.concatenate(split(weights[b]), axis=0), values[b])
        sums = both[:heads] + both[heads:]
        for part in range(per_head):
            packed = jnp.concatenate(
                [sums[:, part * width : (part + 1) * width], tops[b], totals[b]], axis=1
            )
            for h in range(heads):
                out[h * per_head + part, b : b + 1, :] = packed[h : h + 1]
    for load in later:
        load.wait()


def project_kernel(parts, weight, out):
    width = weight.shape[0]
    stat = (LANES - width) // 2
    got = parts[...]
    top = jnp.max(got[:, :, width : width + 1], axis=0)
    factor = jnp.exp(got[:, :, width : width + 1] - top[None])
    total = jnp.sum(factor * got[:, :, width + stat : width + stat + 1], axis=0)
    merged = jnp.sum(factor * got[:, :, :width], axis=0)
    attention = (merged / total).astype(BF16)
    tiles = out.shape[1] // attention.shape[0]
    columns = tiles * LANES
    for piece in range(out.shape[0]):
        term = dot(attention, weight[:, piece * columns : (piece + 1) * columns])
        out[piece] = jnp.concatenate(
            [term[:, tile * LANES : (tile + 1) * LANES] for tile in range(tiles)], axis=0
        ).astype(BF16)


def column_mask(shape, width):
    group = lax.axis_index("kvh")
    lanes = lax.broadcasted_iota(jnp.int32, shape, len(shape) - 1)
    return (lanes >= group * width) & (lanes < (group + 1) * width)


def carry_kernel(parts, residual, out):
    batch = residual.shape[0]
    stacked = jnp.sum(parts[...].astype(F32), axis=0)
    summed = jnp.concatenate(
        [stacked[row : row + batch] for row in range(0, stacked.shape[0], batch)], axis=1
    )
    spread = jnp.concatenate([residual[...]] * (summed.shape[1] // residual.shape[1]), axis=1)
    summed = summed + jnp.where(column_mask(summed.shape, residual.shape[1]), spread, 0.0)
    top = jnp.max(jnp.abs(summed), axis=1, keepdims=True)
    exponent = jnp.ceil(jnp.log2(jnp.maximum(top, 1e-30)))
    width = summed.shape[1]
    out[:, :width] = summed * jnp.exp2(-exponent)
    out[:, width:] = jnp.broadcast_to(exponent, (batch, LANES))


def gate_up_half(scaled, core, gate_weight, up_weight):
    batch = scaled.shape[0]
    terms = jnp.concatenate(split(scaled), axis=0)
    half = gate_weight.shape[1] // CORES
    lanes = pl.ds(pl.multiple_of(core * half, LANES), half)
    gate = dot(terms, gate_weight[:, lanes])
    up = dot(terms, up_weight[:, lanes])
    return jnp.concatenate([gate[:batch] + gate[batch:], up[:batch] + up[batch:]], axis=0)


def gate_give_kernel(
    parts, gain, gate_weight, up_weight, _, give, scaled_out, squares_out, carried_out
):
    batch = parts.shape[1]
    columns = parts.shape[2] - LANES
    carried = sum(
        parts[group, :, :columns] * jnp.exp2(parts[group, :, columns : columns + 1])
        for group in range(parts.shape[0])
    )
    width = carried_out.shape[1]
    own = jnp.where(column_mask(carried.shape, width), carried, 0.0)
    carried_out[...] = sum(
        own[:, piece * width : (piece + 1) * width] for piece in range(carried.shape[1] // width)
    )
    squares = jnp.sum(carried * carried, axis=1, keepdims=True)
    squares = jnp.broadcast_to(jnp.concatenate([squares, squares], axis=0), (2 * batch, LANES))
    scaled = carried * gain[...]
    half = gate_weight.shape[1] // CORES
    give[:, :half] = gate_up_half(scaled, 1 - lax.axis_index("core"), gate_weight, up_weight)
    give[:, half:] = squares
    scaled_out[...] = scaled
    squares_out[...] = squares


def gate_keep_kernel(scaled, squares, gate_weight, up_weight, keep):
    half = gate_weight.shape[1] // CORES
    keep[:, :half] = gate_up_half(scaled[...], lax.axis_index("core"), gate_weight, up_weight)
    keep[:, half:] = squares[...]


def pair_kernel(keep, got, out):
    batch = keep.shape[0] // 2
    summed = keep[...] + got[...]
    half = summed.shape[1] - LANES
    high, low = split(summed[:batch, half:])
    packed = jnp.concatenate(
        [summed[:, :half].astype(BF16), jnp.concatenate([high, low], axis=0)], axis=1
    )
    middle = packed.shape[1] // 2
    packed = jnp.concatenate([packed[:, :middle], packed[:, middle:]], axis=0)
    for piece in range(out.shape[0]):
        out[piece] = packed


def activate_kernel(model_width, parts, out):
    batch = out.shape[0]
    stacked = jnp.sum(parts[...].astype(F32), axis=0)
    rows = stacked.shape[0] // 2
    summed = jnp.concatenate([stacked[:rows], stacked[rows:]], axis=1)
    half = out.shape[1]
    squares = summed[:batch, half : half + 1] + summed[batch:, half : half + 1]
    scale = lax.rsqrt(squares / model_width + EPSILON)
    gate = summed[:batch, :half] * scale
    up = summed[batch:, :half] * scale
    out[...] = (gate / (1.0 + jnp.exp(-gate)) * up).astype(BF16).astype(F32)


def down_half(activated, core, weight):
    half = weight.shape[0] // CORES
    rows = pl.ds(pl.multiple_of(core * half, LANES), half)
    return dot(activated[...].astype(BF16), weight[rows, :])


def down_own_kernel(activated, weight, out):
    out[...] = down_half(activated, lax.axis_index("core"), weight)


def down_kernel(activated, weight, own, out):
    down = own[...] + down_half(activated, 1 - lax.axis_index("core"), weight)
    pieces = out.shape[0]
    width = down.shape[1] // pieces
    per_tile = LANES // width
    for piece in range(pieces):
        tile = down[:, piece // per_tile * LANES : (piece // per_tile + 1) * LANES]
        shift = piece % per_tile * width
        out[piece] = tile if shift == 0 else pltpu.roll(tile, LANES - shift, 1)


def finish_kernel(parts, carried, out):
    out[...] = carried[...] + jnp.sum(parts[...], axis=0)[:, : out.shape[1]]


VMEM = pl.BlockSpec(memory_space=pltpu.VMEM)
HBM = pl.BlockSpec(memory_space=pltpu.HBM)
SHORT = pl.CostEstimate(flops=0, bytes_accessed=2 * 1024 * 1024, transcendentals=0)


def call(kernel, shapes, *args, specs=None, scratch=()):
    return pl.pallas_call(
        kernel,
        out_shape=shapes,
        in_specs=specs or [VMEM] * len(args),
        out_specs=jax.tree.map(lambda _: VMEM, shapes),
        scratch_shapes=scratch,
        cost_estimate=SHORT,
        compiler_params=pltpu.CompilerParams(vmem_limit_bytes=16 * 1024 * 1024),
    )(*args)


def swap(array, axis):
    return lax.all_to_all(array, axis, split_axis=0, concat_axis=0, tiled=True)


def other_core(array):
    return lax.ppermute(array, "core", [(0, 1), (1, 0)])


def on_device(
    query,
    key_cache,
    value_cache,
    lengths,
    residual,
    out_weight,
    norm_gain,
    gate_weight,
    up_weight,
    down_weight,
):
    chips = lax.axis_size("chip")
    shards = chips * CORES
    groups = lax.axis_size("kvh")
    batch = query.shape[0]
    columns = norm_gain.shape[0]
    own = residual.shape[1]
    half = gate_weight.shape[1] // CORES
    padded = half + LANES

    def shape(*dims, dtype=F32):
        return jax.ShapeDtypeStruct(dims, dtype)

    keys = key_cache[:, :, 0, :]
    values = value_cache[:, :, 0, :]
    with jax.named_scope("attend"):
        ahead = (residual, norm_gain.reshape(1, columns))
        operands = [
            pltpu.with_memory_space_constraint(array, pltpu.HBM)
            for array in (lengths, query, keys, values, *ahead, out_weight, gate_weight, up_weight, down_weight)
        ]
        partial, residual, gain = call(
            functools.partial(attend_kernel, batch),
            (
                shape(shards, batch, LANES),
                *(pltpu.VMEM(array.shape, array.dtype) for array in ahead),
            ),
            *operands,
            specs=[HBM] * len(operands),
            scratch=[
                pltpu.SMEM(lengths.shape, lengths.dtype),
                pltpu.VMEM(query.shape, query.dtype),
                pltpu.VMEM(keys.shape, keys.dtype),
                pltpu.VMEM(values.shape, values.dtype),
                pltpu.SemaphoreType.DMA((4 + len(ahead),)),
            ],
        )
    partial = swap(partial, ("chip", "core"))
    with jax.named_scope("project"):
        projected = call(
            project_kernel,
            shape(shards, batch * columns // LANES, LANES, dtype=BF16),
            partial,
            out_weight[0],
        )
    projected = swap(projected, ("chip", "core"))
    with jax.named_scope("carry"):
        carried = call(carry_kernel, shape(batch, columns + LANES), projected, residual)
    carried = jnp.broadcast_to(carried.astype(jnp.float16)[None], (groups, *carried.shape))
    carried = swap(carried, "kvh").astype(F32)
    with jax.named_scope("gate_up_give"):
        give, scaled, squares, own_carried = call(
            gate_give_kernel,
            (
                shape(2 * batch, padded),
                shape(batch, columns),
                shape(2 * batch, LANES),
                shape(batch, own),
            ),
            carried,
            gain,
            gate_weight,
            up_weight,
            down_weight,
        )
    got = other_core(give)
    with jax.named_scope("gate_up_keep"):
        keep = call(
            gate_keep_kernel, shape(2 * batch, padded), scaled, squares, gate_weight, up_weight
        )
    with jax.named_scope("pair"):
        hidden = call(pair_kernel, shape(chips, 4 * batch, padded // 2, dtype=BF16), keep, got)
    hidden = swap(hidden, "chip")
    with jax.named_scope("activate"):
        model_width = shards * columns
        activated = call(
            functools.partial(activate_kernel, model_width), shape(batch, half), hidden
        )
    other = other_core(activated)
    with jax.named_scope("down_own"):
        down = call(down_own_kernel, shape(batch, columns), activated, down_weight)
    with jax.named_scope("down"):
        down = call(down_kernel, shape(groups, batch, LANES), other, down_weight, down)
    down = swap(down, "kvh")
    with jax.named_scope("finish"):
        return call(finish_kernel, shape(batch, own), down, own_carried)


def solution(mesh):
    seq, kvh = mesh.devices.shape
    chips = Mesh(mesh.devices.reshape(seq // CORES, CORES, kvh), ("chip", "core", "kvh"))
    shard = ("chip", "core")
    return jax.shard_map(
        on_device,
        mesh=chips,
        in_specs=(
            P(None, "kvh", None),
            P(None, shard, "kvh", None),
            P(None, shard, "kvh", None),
            P(),
            P(None, (*shard, "kvh")),
            P("kvh", shard, None),
            P(shard),
            P(shard, "kvh"),
            P(shard, "kvh"),
            P("kvh", shard),
        ),
        out_specs=P(None, (*shard, "kvh")),
        check_vma=False,
    )
```

```python
import functools

import jax
import jax.numpy as jnp
from jax import lax
from jax.experimental import pallas as pl
from jax.experimental.pallas import tpu as pltpu
from jax.sharding import Mesh, PartitionSpec as P

EPSILON = 1e-05
MASKED = -1e30
LANES = 128
CORES = 2
F32 = jnp.float32
BF16 = jnp.bfloat16


def dot(a, b):
    return jnp.dot(a, b, preferred_element_type=F32)


def split(array):
    high = array.astype(BF16)
    return high, (array - high.astype(F32)).astype(BF16)


def attend_kernel(batch, *refs):
    lengths_hbm, query_hbm, keys_hbm, values_hbm = refs[:4]
    ahead = (len(refs) - 14) // 2
    out = refs[8 + ahead]
    lengths, query, keys, values, sems = refs[-5:]
    later = [
        pltpu.make_async_copy(refs[4 + i], refs[9 + ahead + i], sems.at[4 + i])
        for i in range(ahead)
    ]
    heads, head_dim = query.shape[1:]
    positions_here = keys.shape[1]
    loads = [
        pltpu.make_async_copy(lengths_hbm, lengths, sems.at[0]),
        pltpu.make_async_copy(query_hbm, query, sems.at[1]),
    ]
    key_load = pltpu.make_async_copy(keys_hbm, keys, sems.at[2])
    value_load = pltpu.make_async_copy(values_hbm, values, sems.at[3])
    for load in (*loads, key_load, value_load, *later):
        load.start()
    for load in loads:
        load.wait()
    pieces = out.shape[0]
    per_head = pieces // heads
    width = head_dim // per_head
    stat = (LANES - width) // 2
    shard = lax.axis_index("chip") * CORES + lax.axis_index("core")
    positions = shard * positions_here + lax.broadcasted_iota(jnp.int32, (heads, positions_here), 1)
    weights, tops, totals = [], [], []
    key_load.wait()
    for b in range(batch):
        scores = lax.dot_general(
            query[b], keys[b], (((1,), (1,)), ((), ())), preferred_element_type=F32
        ) * head_dim ** (-0.5)
        live = positions < lengths[b]
        masked = jnp.where(live, scores, MASKED)
        top = jnp.max(masked, axis=1, keepdims=True)
        weights.append(jnp.where(live, jnp.exp(masked - top), 0.0))
        tops.append(jnp.broadcast_to(top, (heads, stat)))
        totals.append(jnp.broadcast_to(jnp.sum(weights[b], axis=1, keepdims=True), (heads, stat)))
    value_load.wait()
    for b in range(batch):
        both = dot(jnp.concatenate(split(weights[b]), axis=0), values[b])
        sums = both[:heads] + both[heads:]
        for part in range(per_head):
            packed = jnp.concatenate(
                [sums[:, part * width : (part + 1) * width], tops[b], totals[b]], axis=1
            )
            for h in range(heads):
                out[h * per_head + part, b : b + 1, :] = packed[h : h + 1]
    for load in later:
        load.wait()


def project_kernel(parts, weight, out):
    width = weight.shape[0]
    stat = (LANES - width) // 2
    got = parts[...]
    top = jnp.max(got[:, :, width : width + 1], axis=0)
    factor = jnp.exp(got[:, :, width : width + 1] - top[None])
    total = jnp.sum(factor * got[:, :, width + stat : width + stat + 1], axis=0)
    merged = jnp.sum(factor * got[:, :, :width], axis=0)
    attention = (merged / total).astype(BF16)
    tiles = out.shape[1] // attention.shape[0]
    columns = tiles * LANES
    for piece in range(out.shape[0]):
        term = dot(attention, weight[:, piece * columns : (piece + 1) * columns])
        out[piece] = jnp.concatenate(
            [term[:, tile * LANES : (tile + 1) * LANES] for tile in range(tiles)], axis=0
        ).astype(BF16)


def column_mask(shape, width):
    group = lax.axis_index("kvh")
    lanes = lax.broadcasted_iota(jnp.int32, shape, len(shape) - 1)
    return (lanes >= group * width) & (lanes < (group + 1) * width)


def carry_kernel(parts, residual, out):
    batch = residual.shape[0]
    stacked = jnp.sum(parts[...].astype(F32), axis=0)
    summed = jnp.concatenate(
        [stacked[row : row + batch] for row in range(0, stacked.shape[0], batch)], axis=1
    )
    spread = jnp.concatenate([residual[...]] * (summed.shape[1] // residual.shape[1]), axis=1)
    summed = summed + jnp.where(column_mask(summed.shape, residual.shape[1]), spread, 0.0)
    for piece in range(out.shape[0]):
        out[piece] = summed


def gate_up_half(scaled, core, gate_weight, up_weight):
    batch = scaled.shape[0]
    terms = jnp.concatenate(split(scaled), axis=0)
    half = gate_weight.shape[1] // CORES
    lanes = pl.ds(pl.multiple_of(core * half, LANES), half)
    gate = dot(terms, gate_weight[:, lanes])
    up = dot(terms, up_weight[:, lanes])
    return jnp.concatenate([gate[:batch] + gate[batch:], up[:batch] + up[batch:]], axis=0)


def square_sums(carried):
    sums = jnp.sum(carried * carried, axis=1, keepdims=True)
    return jnp.broadcast_to(
        jnp.concatenate([sums, sums], axis=0), (2 * carried.shape[0], LANES)
    )


def gate_give_kernel(parts, gain, gate_weight, up_weight, _, give, carried_out):
    carried = jnp.sum(parts[...], axis=0)
    carried_out[...] = carried
    half = gate_weight.shape[1] // CORES
    give[:, :half] = gate_up_half(
        carried * gain[...], 1 - lax.axis_index("core"), gate_weight, up_weight
    )
    give[:, half:] = square_sums(carried)


def gate_keep_kernel(carried_in, gain, gate_weight, up_weight, keep, own_out):
    carried = carried_in[...]
    half = gate_weight.shape[1] // CORES
    keep[:, :half] = gate_up_half(
        carried * gain[...], lax.axis_index("core"), gate_weight, up_weight
    )
    keep[:, half:] = square_sums(carried)
    width = own_out.shape[1]
    own = jnp.where(column_mask(carried.shape, width), carried, 0.0)
    own_out[...] = sum(
        own[:, piece * width : (piece + 1) * width] for piece in range(carried.shape[1] // width)
    )


def pair_kernel(keep, got, out):
    batch = keep.shape[0] // 2
    summed = keep[...] + got[...]
    half = summed.shape[1] - LANES
    high, low = split(summed[:batch, half:])
    packed = jnp.concatenate(
        [summed[:, :half].astype(BF16), jnp.concatenate([high, low], axis=0)], axis=1
    )
    middle = packed.shape[1] // 2
    packed = jnp.concatenate([packed[:, :middle], packed[:, middle:]], axis=0)
    for piece in range(out.shape[0]):
        out[piece] = packed


def activate_kernel(model_width, parts, out):
    batch = out.shape[0]
    stacked = jnp.sum(parts[...].astype(F32), axis=0)
    rows = stacked.shape[0] // 2
    summed = jnp.concatenate([stacked[:rows], stacked[rows:]], axis=1)
    half = out.shape[1]
    squares = summed[:batch, half : half + 1] + summed[batch:, half : half + 1]
    scale = lax.rsqrt(squares / model_width + EPSILON)
    gate = summed[:batch, :half] * scale
    up = summed[batch:, :half] * scale
    out[...] = (gate / (1.0 + jnp.exp(-gate)) * up).astype(BF16).astype(F32)


def down_half(activated, core, weight):
    half = weight.shape[0] // CORES
    rows = pl.ds(pl.multiple_of(core * half, LANES), half)
    return dot(activated[...].astype(BF16), weight[rows, :])


def down_own_kernel(activated, weight, out):
    out[...] = down_half(activated, lax.axis_index("core"), weight)


def down_kernel(activated, weight, own, out):
    down = own[...] + down_half(activated, 1 - lax.axis_index("core"), weight)
    pieces = out.shape[0]
    width = down.shape[1] // pieces
    per_tile = LANES // width
    for piece in range(pieces):
        tile = down[:, piece // per_tile * LANES : (piece // per_tile + 1) * LANES]
        shift = piece % per_tile * width
        out[piece] = tile if shift == 0 else pltpu.roll(tile, LANES - shift, 1)


def finish_kernel(parts, carried, out):
    out[...] = carried[...] + jnp.sum(parts[...], axis=0)[:, : out.shape[1]]


VMEM = pl.BlockSpec(memory_space=pltpu.VMEM)
HBM = pl.BlockSpec(memory_space=pltpu.HBM)
SHORT = pl.CostEstimate(flops=0, bytes_accessed=2 * 1024 * 1024, transcendentals=0)


def call(kernel, shapes, *args, specs=None, scratch=()):
    return pl.pallas_call(
        kernel,
        out_shape=shapes,
        in_specs=specs or [VMEM] * len(args),
        out_specs=jax.tree.map(lambda _: VMEM, shapes),
        scratch_shapes=scratch,
        cost_estimate=SHORT,
        compiler_params=pltpu.CompilerParams(vmem_limit_bytes=16 * 1024 * 1024),
    )(*args)


def swap(array, axis):
    return lax.all_to_all(array, axis, split_axis=0, concat_axis=0, tiled=True)


def other_core(array):
    return lax.ppermute(array, "core", [(0, 1), (1, 0)])


def on_device(
    query,
    key_cache,
    value_cache,
    lengths,
    residual,
    out_weight,
    norm_gain,
    gate_weight,
    up_weight,
    down_weight,
):
    chips = lax.axis_size("chip")
    shards = chips * CORES
    groups = lax.axis_size("kvh")
    batch = query.shape[0]
    columns = norm_gain.shape[0]
    own = residual.shape[1]
    half = gate_weight.shape[1] // CORES
    padded = half + LANES

    def shape(*dims, dtype=F32):
        return jax.ShapeDtypeStruct(dims, dtype)

    keys = key_cache[:, :, 0, :]
    values = value_cache[:, :, 0, :]
    with jax.named_scope("attend"):
        ahead = (residual, norm_gain.reshape(1, columns))
        operands = [
            pltpu.with_memory_space_constraint(array, pltpu.HBM)
            for array in (lengths, query, keys, values, *ahead, out_weight, gate_weight, up_weight, down_weight)
        ]
        partial, residual, gain = call(
            functools.partial(attend_kernel, batch),
            (
                shape(shards, batch, LANES),
                *(pltpu.VMEM(array.shape, array.dtype) for array in ahead),
            ),
            *operands,
            specs=[HBM] * len(operands),
            scratch=[
                pltpu.SMEM(lengths.shape, lengths.dtype),
                pltpu.VMEM(query.shape, query.dtype),
                pltpu.VMEM(keys.shape, keys.dtype),
                pltpu.VMEM(values.shape, values.dtype),
                pltpu.SemaphoreType.DMA((4 + len(ahead),)),
            ],
        )
    partial = swap(partial, ("chip", "core"))
    with jax.named_scope("project"):
        projected = call(
            project_kernel,
            shape(shards, batch * columns // LANES, LANES, dtype=BF16),
            partial,
            out_weight[0],
        )
    projected = swap(projected, ("chip", "core"))
    with jax.named_scope("carry"):
        carried = call(carry_kernel, shape(groups, batch, columns), projected, residual)
    carried = swap(carried, "kvh")
    with jax.named_scope("gate_up_give"):
        give, carried = call(
            gate_give_kernel,
            (shape(2 * batch, padded), shape(batch, columns)),
            carried,
            gain,
            gate_weight,
            up_weight,
            down_weight,
        )
    got = other_core(give)
    with jax.named_scope("gate_up_keep"):
        keep, own_carried = call(
            gate_keep_kernel,
            (shape(2 * batch, padded), shape(batch, own)),
            carried,
            gain,
            gate_weight,
            up_weight,
        )
    with jax.named_scope("pair"):
        hidden = call(pair_kernel, shape(chips, 4 * batch, padded // 2, dtype=BF16), keep, got)
    hidden = swap(hidden, "chip")
    with jax.named_scope("activate"):
        model_width = shards * columns
        activated = call(
            functools.partial(activate_kernel, model_width), shape(batch, half), hidden
        )
    other = other_core(activated)
    with jax.named_scope("down_own"):
        down = call(down_own_kernel, shape(batch, columns), activated, down_weight)
    with jax.named_scope("down"):
        down = call(down_kernel, shape(groups, batch, LANES), other, down_weight, down)
    down = swap(down, "kvh")
    with jax.named_scope("finish"):
        return call(finish_kernel, shape(batch, own), down, own_carried)


def solution(mesh):
    seq, kvh = mesh.devices.shape
    chips = Mesh(mesh.devices.reshape(seq // CORES, CORES, kvh), ("chip", "core", "kvh"))
    shard = ("chip", "core")
    return jax.shard_map(
        on_device,
        mesh=chips,
        in_specs=(
            P(None, "kvh", None),
            P(None, shard, "kvh", None),
            P(None, shard, "kvh", None),
            P(),
            P(None, (*shard, "kvh")),
            P("kvh", shard, None),
            P(shard),
            P(shard, "kvh"),
            P(shard, "kvh"),
            P("kvh", shard),
        ),
        out_specs=P(None, (*shard, "kvh")),
        check_vma=False,
    )
```
